32 devices in a mesh: ctx: 4 (over z), exp: 8 (over y, x, core).
Axes of the slice: x: 2, y: 2, z: 4, core: 2. Of those that a mesh axis runs over, the one named last changes fastest.
Arguments:
- queries: bfloat16 [8, 256, 1024], P('exp', 'ctx'), may hold values from -6 to 6
- keys: bfloat16 [8, 256, 1024], P('exp', 'ctx'), may hold values from -6 to 6
- values: bfloat16 [8, 256, 1024], P('exp', 'ctx'), may hold values from -6 to 6
- residual: bfloat16 [8, 256, 2048], P('exp', 'ctx'), may hold values from -6 to 6
- out_proj: bfloat16 [1024, 2048], replicated, may hold values from -0.1875 to 0.1875
- norm_gain: float32 [2048], replicated, may hold values from 0.25 to 1.75
- w_gate: bfloat16 [8, 2048, 512], P('exp'), may hold values from -0.125 to 0.125
- w_up: bfloat16 [8, 2048, 512], P('exp'), may hold values from -0.125 to 0.125
- w_down: bfloat16 [8, 512, 2048], P('exp'), may hold values from -0.25 to 0.25
- routes: int32 [8, 256, 4], P('exp', 'ctx'), may hold values from 0 to 7, all different within a row; in each aligned block of 64 rows (0 to 63, 64 to 127, ..., all dimensions but the last counted through in order) at most 48 rows name the same one
- route_prob: float32 [8, 256, 4], P('exp', 'ctx'), may hold values from 0.05 to 0.8
Outputs:
- mixed: bfloat16 [8, 256, 2048], P('exp', 'ctx')
The draws below stay inside these ranges and needn't reach their ends.
Inputs may be any that keep to these rules, and one draw needn't show every extreme that they name: `routes`: each row names 4 different experts; the 64 rows of one device name no expert more than 48 times, and in some devices' rows one expert exactly 48 times.
All inputs are finite; a program needn't handle non-finite values.
Results may differ from the reference program's by a relative error of at most 0.008.
Values may be sent and summed in bfloat16 or wider, within the bound.
A program may use at most 64 MiB of HBM per device.

```python
import math
import jax
import jax.numpy as jnp
import numpy as np
from jax import lax

D = 2048
HEADS = 8
HEAD_DIM = 128
FFW = 512
TOP = 4
TOK_DEV = 64
SEQS = 8
LEN = 256
EXPERTS = 8
CAP = 48
N_CTX = 4


def drawn_draw(key):
    full_shape = (SEQS, LEN, HEADS * HEAD_DIM)
    return jnp.clip(1.6 * jax.random.normal(key, full_shape, jnp.float32), -6.0, 6.0)


def draw_queries(key, part):
    drawn = drawn_draw(jax.random.fold_in(key, 1))
    return drawn.astype(jnp.bfloat16)


def draw_keys(key, part):
    drawn = drawn_draw(jax.random.fold_in(key, 2))
    return drawn.astype(jnp.bfloat16)


def level_of(own_key, shape, shards, smallest, largest):
    def one(dim, shards_of):
        heights = jax.random.uniform(jax.random.fold_in(jax.random.fold_in(own_key, 6), dim), (shards_of,), jnp.float32, smallest / len(shards), largest / len(shards))
        return jnp.repeat(jnp.exp(heights), shape[dim] // shards_of).reshape((-1,) + (1,) * (len(shape) - dim - 1))

    gain = one(*shards[0])
    for cut in shards[1:]:
        gain = gain * one(*cut)
    return gain


def assign_block(key, own, number, rows, count, top, limit, skew):
    order = jax.random.permutation(key, count)
    packed, ordinary = portions_of(count, rows * top, limit, skew, True), portions_of(count, rows * top, limit, skew, False)
    places = jnp.arange(count)

    def named(sizes, rotation):
        used = int((sizes > 0).sum())
        fixed = max(1, used // 4)
        moved = fixed + (places - fixed + rotation * (used - fixed)) % max(1, count - fixed)
        return jnp.zeros((count,), jnp.int32).at[order[jnp.where(places < fixed, places, moved)]].set(jnp.asarray(sizes, jnp.int32))

    sizes = jnp.where(number % 4 == 0, named(packed, number // 4), named(ordinary, number - number // 4 - 1))
    mixed = jax.random.permutation(jax.random.fold_in(own, 3), count)
    giver, taker = mixed[0:count // 2 * 2:2], mixed[1:count // 2 * 2:2]
    slack = jnp.minimum(sizes[giver] - 1, limit - sizes[taker]) // 2
    slack = jnp.where((giver == order[0]) | (taker == order[0]) | (sizes[taker] == 0), 0, jnp.maximum(slack, 0))
    moved = jax.random.randint(jax.random.fold_in(own, 4), (count // 2,), 0, 1 << 20) % (slack + 1)
    sizes = sizes.at[giver].add(-moved).at[taker].add(moved)
    items = jnp.searchsorted(jnp.cumsum(sizes), jnp.arange(rows * top), side="right").astype(jnp.int32)
    table = items.reshape(top, rows).T
    table = table[jax.random.permutation(jax.random.fold_in(own, 1), rows)]
    rotation = jax.random.randint(jax.random.fold_in(own, 2), (rows, 1), 0, top)
    return jnp.take_along_axis(table, (jnp.arange(top)[None, :] + rotation) % top, axis=1)


def portions_of(count, total, reach, lean, full):
    portions = [(1 << 20) // math.isqrt(standing ** lean) + 1 for standing in range(1, count + 1)]
    largest = reach if full else min(reach, max(-(-total // count), total * portions[0] // sum(portions)))
    least = 1 if total - largest >= count - 1 else 0
    counts, rest = [largest] + [least] * (count - 1), total - largest - least * (count - 1)
    while rest > 0:
        free = [i for i in range(1, count) if counts[i] < largest] or [i for i in range(1, count) if counts[i] < reach]
        mass, remaining = sum([portions[i] for i in free]), rest
        for i in free:
            more = min(reach - counts[i], max(1, remaining * portions[i] // mass), rest)
            counts[i] = counts[i] + more
            rest = rest - more
    return np.array(counts)


def scatter_about(own_key, dims, width, bound, cuts=(), held_as=jnp.bfloat16):
    values = width * jax.random.normal(own_key, dims, jnp.float32)
    if cuts:
        values = values * level_of(own_key, dims, cuts, -0.22, 0.18)
    return jnp.clip(values, -bound, bound).astype(held_as)


def setup_inputs(seed: int = 0) -> dict:
    splits = jax.random.split(jax.random.key(seed), 12)
    queries = draw_queries(jax.random.fold_in(splits[11], 71), 0)
    keys = draw_keys(jax.random.fold_in(splits[11], 71), 0)
    values = scatter_about(splits[2], (SEQS, LEN, HEADS * HEAD_DIM), 1.0, 6.0, ((0, 8), (1, 4)))
    residual = scatter_about(splits[3], (SEQS, LEN, D), 1.0, 6.0, ((0, 8), (1, 4)))
    out_proj = scatter_about(splits[4], (HEADS * HEAD_DIM, D), (HEADS * HEAD_DIM) ** -0.5, 0.1875)
    norm_gain = jnp.clip(1.0 + 0.15 * jax.random.normal(splits[5], (D,), jnp.float32), 0.25, 1.75)
    w_gate = scatter_about(splits[6], (EXPERTS, D, FFW), D ** -0.5, 0.125, ((0, 8),))
    w_up = scatter_about(splits[7], (EXPERTS, D, FFW), D ** -0.5, 0.125, ((0, 8),))
    w_down = scatter_about(splits[8], (EXPERTS, FFW, D), FFW ** -0.5, 0.25, ((0, 8),))
    routes_keys = jax.random.split(jax.random.fold_in(splits[9], 1), SEQS * LEN // TOK_DEV)
    routes_turns = jax.random.permutation(jax.random.fold_in(splits[9], 3), SEQS * LEN // TOK_DEV)
    routes = jax.vmap(lambda own, number: assign_block(jax.random.fold_in(splits[9], 2), own, number, TOK_DEV, EXPERTS, TOP, CAP, 2))(routes_keys, routes_turns).reshape((SEQS, LEN, TOP))
    route_prob = jnp.clip(jnp.exp(math.log(0.8) - 2.7725887 * jax.random.uniform(splits[10], (SEQS, LEN, TOP), jnp.float32) ** level_of(splits[10], (SEQS, LEN, TOP), ((0, 8), (1, 4)), -0.2, 0.2)), 0.05, 0.8)
    return dict(queries=queries, keys=keys, values=values, residual=residual, out_proj=out_proj, norm_gain=norm_gain, w_gate=w_gate, w_up=w_up, w_down=w_down, routes=routes, route_prob=route_prob)


def attend_sequence(inputs):
    query_seq, key_seq, value_seq = inputs
    length = query_seq.shape[0]
    query_float = query_seq.astype(jnp.float32).reshape(length, HEADS, HEAD_DIM)
    key_float = key_seq.astype(jnp.float32).reshape(length, HEADS, HEAD_DIM)
    value_float = value_seq.astype(jnp.float32).reshape(length, HEADS, HEAD_DIM)
    scores = jnp.einsum('qhd,khd->hqk', query_float, key_float) * HEAD_DIM ** (-0.5)
    positions = jnp.arange(length, dtype=jnp.int32)
    allowed = positions[None, :] <= positions[:, None]
    scores = jnp.where(allowed[None], scores, -1e+30)
    row_max = scores.max(axis=-1, keepdims=True)
    exponent = jnp.where(allowed[None], jnp.exp(scores - row_max), 0.0)
    denom = exponent.sum(axis=-1)
    rounded = lax.optimization_barrier(exponent.astype(jnp.bfloat16)).astype(jnp.float32)
    output = jnp.einsum('hqk,khd->qhd', rounded, value_float) / jnp.transpose(denom)[:, :, None]
    return output.reshape(length, HEADS * HEAD_DIM).astype(jnp.bfloat16)

def reference(queries, keys, values, residual, out_proj, norm_gain, w_gate, w_up, w_down, routes, route_prob):
    attended = lax.map(attend_sequence, (queries, keys, values))
    projected = jnp.dot(attended.reshape(-1, HEADS * HEAD_DIM), out_proj, preferred_element_type=jnp.float32)
    hidden = residual.astype(jnp.float32).reshape(-1, D) + projected
    mean_square = lax.optimization_barrier(jnp.mean(hidden * hidden, axis=-1, keepdims=True))
    normed = (hidden * lax.rsqrt(mean_square + 1e-05) * norm_gain).astype(jnp.bfloat16)
    chosen = routes.reshape(-1)
    prob_flat = route_prob.reshape(-1)
    most_rows = SEQS * N_CTX * CAP

    def per_expert(totals, expert_inputs):
        expert_id, gate_mat, up_mat, down_mat = expert_inputs
        matches = chosen == expert_id
        found = jnp.nonzero(matches, size=most_rows, fill_value=0)[0].astype(jnp.int32)
        live = jnp.arange(most_rows, dtype=jnp.int32) < jnp.sum(matches.astype(jnp.int32))
        token_rows = found // TOP
        gathered = normed[token_rows]
        gate_part = jnp.dot(gathered, gate_mat, preferred_element_type=jnp.float32)
        up_part = jnp.dot(gathered, up_mat, preferred_element_type=jnp.float32)
        activated = (jax.nn.silu(gate_part) * up_part).astype(jnp.bfloat16)
        produced = jnp.dot(activated, down_mat, preferred_element_type=jnp.float32).astype(jnp.bfloat16)
        produced = lax.optimization_barrier(produced).astype(jnp.float32)
        factor = jnp.where(live, prob_flat[found], 0.0)
        totals = totals.at[token_rows].add(factor[:, None] * produced)
        return (totals, None)
    start_totals = jnp.zeros((chosen.shape[0] // TOP, D), jnp.float32)
    expert_ids = jnp.arange(EXPERTS, dtype=jnp.int32)
    totals, unused = lax.scan(per_expert, start_totals, (expert_ids, w_gate, w_up, w_down))
    return (hidden + totals).astype(jnp.bfloat16).reshape(residual.shape)
```

```python
import functools

import jax
import jax.numpy as jnp
from jax import lax
from jax.experimental import pallas as pl
from jax.experimental.pallas import tpu as pltpu
from jax.sharding import PartitionSpec as P

HEADS = 8
HEAD_DIM = 128
TOP = 4


neg_big = -1e30


def passed_along(block, axis, distance):
    devices = range(lax.axis_size(axis))
    route = [(i - distance, i) for i in devices if i - distance in devices]
    return lax.ppermute(block, axis, route)


def attend_piece(softmax_state, query_heads, query_pos, key_piece, piece_start):
    run_max, run_sum, run_acc = softmax_state
    length = key_piece.shape[1]
    key_rows = key_piece[0].reshape(length, HEADS, HEAD_DIM)
    value_rows = key_piece[1].reshape(length, HEADS, HEAD_DIM)
    scale = HEAD_DIM ** (-0.5)
    scores = jnp.einsum("hqd,khd->hqk", query_heads, key_rows, preferred_element_type=jnp.float32)
    key_pos = piece_start + jnp.arange(length, dtype=jnp.int32)
    allowed = key_pos[None, :] <= query_pos[:, None]
    scores = jnp.where(allowed[None], scores, neg_big)
    new_max = jnp.maximum(run_max, scores.max(axis=-1))
    rescale = jnp.exp((run_max - new_max) * scale)
    exponent = jnp.where(allowed[None], jnp.exp((scores - new_max[:, :, None]) * scale), 0.0)
    run_sum = run_sum * rescale + exponent.sum(axis=-1)
    update = jnp.einsum(
        "hqk,khd->hqd",
        exponent.astype(jnp.bfloat16),
        value_rows,
        preferred_element_type=jnp.float32,
    )
    run_acc = run_acc * rescale[:, :, None] + update
    return (new_max, run_sum, run_acc)


def local(
    queries, keys, values, residual, out_proj, norm_gain, w_gate, w_up, w_down, routes, route_prob
):
    tok_count = queries.shape[1]
    my_index = lax.axis_index("ctx")
    query_pos = my_index * tok_count + jnp.arange(tok_count, dtype=jnp.int32)
    query_heads = jnp.transpose(queries[0].reshape(tok_count, HEADS, HEAD_DIM), (1, 0, 2))
    stacked = jnp.stack([keys[0], values[0]])
    start_state = (
        jnp.full((HEADS, tok_count), neg_big, jnp.float32),
        jnp.zeros((HEADS, tok_count), jnp.float32),
        jnp.zeros((HEADS, tok_count, HEAD_DIM), jnp.float32),
    )
    first_state = attend_piece(start_state, query_heads, query_pos, stacked, my_index * tok_count)

    def advance(offset, loop_carry):
        softmax_state, travelling = loop_carry
        travelling = passed_along(travelling, "ctx", 1)

        def compute(current):
            return attend_piece(
                current, query_heads, query_pos, travelling, (my_index - offset) * tok_count
            )

        def unchanged(current):
            return current

        softmax_state = lax.cond(offset <= my_index, compute, unchanged, softmax_state)
        return (softmax_state, travelling)

    final_state, leftover = lax.fori_loop(1, lax.axis_size("ctx"), advance, (first_state, stacked))
    run_max, run_sum, run_acc = final_state
    attended_heads = (run_acc / run_sum[:, :, None]).astype(jnp.bfloat16)
    attended = jnp.transpose(attended_heads, (1, 0, 2)).reshape(tok_count, HEADS * HEAD_DIM)
    hidden = residual[0].astype(jnp.float32) + jnp.dot(
        attended, out_proj, preferred_element_type=jnp.float32
    )
    mean_square = jnp.mean(hidden * hidden, axis=-1, keepdims=True)
    normed = (hidden * lax.rsqrt(mean_square + 1e-05) * norm_gain).astype(jnp.bfloat16)
    owners = lax.axis_size("exp")
    capacity = 3 * tok_count * TOP // (2 * owners)
    chosen = routes[0].reshape(-1)
    one_hot = (chosen[:, None] == jnp.arange(owners, dtype=jnp.int32)[None, :]).astype(jnp.int32)
    earlier = jnp.cumsum(one_hot, axis=0) - one_hot
    slot_index = jnp.sum(earlier * one_hot, axis=1)
    target = chosen * capacity + slot_index
    token_index = jnp.arange(tok_count * TOP, dtype=jnp.int32) // TOP
    slot_token = jnp.full((owners * capacity,), tok_count, jnp.int32).at[target].set(token_index)
    padded = jnp.concatenate([normed, jnp.zeros((1, normed.shape[1]), jnp.bfloat16)], axis=0)
    outgoing = padded[slot_token].reshape(owners, capacity, normed.shape[1])
    incoming = lax.all_to_all(outgoing, "exp", split_axis=0, concat_axis=0, tiled=True)
    sources, item_count, feature_width = incoming.shape
    flat_rows = incoming.reshape(sources * item_count, feature_width)
    gate_part = jnp.dot(flat_rows, w_gate[0], preferred_element_type=jnp.float32)
    up_part = jnp.dot(flat_rows, w_up[0], preferred_element_type=jnp.float32)
    activated = (jax.nn.silu(gate_part) * up_part).astype(jnp.bfloat16)
    produced = jnp.dot(activated, w_down[0], preferred_element_type=jnp.float32).astype(
        jnp.bfloat16
    )
    produced = produced.reshape(sources, item_count, feature_width)
    returned = lax.all_to_all(produced, "exp", split_axis=0, concat_axis=0, tiled=True)
    picked = (
        returned.reshape(owners * capacity, -1)[target]
        .astype(jnp.float32)
        .reshape(tok_count, TOP, -1)
    )
    mixture = jnp.sum(route_prob[0][:, :, None] * picked, axis=1)
    return (hidden + mixture).astype(jnp.bfloat16)[None]


MESH = pl.DeviceIdType.MESH


def fused_kernel(
    n, chips, q_hbm, k_hbm, v_hbm, res_hbm, wo_hbm, gain_ref, wg_hbm, wu_hbm, wd_hbm, routes_ref, prob_ref,
    out_ref,
    qkv, att, attg, resg, probg, wo, wg, wu, wd, kept, hidden, own, psend, precv, ssend, srecv,
    load_sem, qkv_s, qkv_r, back_s, back_r, near_s, near_r, fwd_s, fwd_r, pair_s, pair_r, sum_s, sum_r,
):
    z = lax.axis_index("ctx")
    me = lax.axis_index("exp")
    core = lax.rem(me, 2)
    chip = me // 2
    partner = me + 1 - 2 * core
    toks = q_hbm.shape[1]
    width = qkv.shape[-1]
    heads_here = width // HEAD_DIM

    def across(d):
        there = chip
        for b in range(chips.bit_length() - 1):
            if (d >> b) & 1:
                there = there + (1 << b) * (1 - 2 * lax.rem(chip // (1 << b), 2))
        return 2 * there + core

    def remote(src, dst, ssem, rsem, **to):
        return pltpu.make_async_remote_copy(
            src_ref=src, dst_ref=dst, send_sem=ssem, recv_sem=rsem, device_id=to, device_id_type=MESH
        )

    def columns(j):
        return pl.ds(pl.multiple_of(j * width, width), width)

    sources = (q_hbm, k_hbm, v_hbm)
    started = []

    def go(copy):
        copy.start()
        started.append(copy)
        return copy

    own_qkv = []
    for t in range(3):
        own_qkv.append(pltpu.make_async_copy(sources[t].at[0, :, columns(z)], qkv.at[t, z], load_sem.at[t]))
        own_qkv[-1].start()
    own_res = pltpu.make_async_copy(res_hbm.at[0], resg.at[0, 0], load_sem.at[3])
    own_res.start()
    loads = []
    for i, (src, dst) in enumerate(((wo_hbm, wo), (wg_hbm.at[0], wg), (wu_hbm.at[0], wu), (wd_hbm.at[0], wd))):
        loads.append(pltpu.make_async_copy(src, dst, load_sem.at[4 + i]))
        loads[-1].start()

    barrier = pltpu.get_barrier_semaphore()
    for d in range(1, n):
        pl.semaphore_signal(barrier, inc=1, device_id={"ctx": lax.rem(z + d, n)}, device_id_type=MESH)
    for d in range(1, chips):
        pl.semaphore_signal(barrier, inc=1, device_id={"exp": across(d)}, device_id_type=MESH)
    pl.semaphore_signal(barrier, inc=1, device_id={"exp": partner}, device_id_type=MESH)
    pl.semaphore_wait(barrier, n - 1 + chips)

    for t in range(3):
        for d in range(1, n):
            j = lax.rem(z + d, n)
            go(remote(sources[t].at[0, :, columns(j)], qkv.at[t, z], qkv_s.at[t, j], qkv_r.at[t, z], ctx=j))
    go(remote(res_hbm.at[0], resg.at[0, 1], near_s.at[0, 0], near_r.at[0, 0], exp=partner))
    for d in range(1, chips):
        go(remote(res_hbm.at[0], resg.at[d, 0], near_s.at[0, d], near_r.at[0, d], exp=across(d)))
    lanes = lax.broadcasted_iota(jnp.int32, probg.shape[2:], 1)
    dense = jnp.zeros(probg.shape[2:], jnp.float32)
    for t in range(TOP):
        dense = dense + jnp.where(lanes == routes_ref[0, :, t : t + 1], prob_ref[0, :, t : t + 1], 0.0)
    probg[0, 0] = dense
    go(remote(probg.at[0, 0], probg.at[0, 1], near_s.at[1, 0], near_r.at[1, 0], exp=partner))
    for d in range(1, chips):
        go(remote(probg.at[0, 0], probg.at[d, 0], near_s.at[1, d], near_r.at[1, d], exp=across(d)))

    for t in range(3):
        own_qkv[t].wait()
        for d in range(1, n):
            s = lax.rem(z + d, n)
            remote(qkv.at[t, s], qkv.at[t, s], qkv_s.at[t, s], qkv_r.at[t, s], ctx=s).wait_recv()
    length = n * toks
    row = lax.broadcasted_iota(jnp.int32, (length, length), 0)
    col = lax.broadcasted_iota(jnp.int32, (length, length), 1)
    for h in range(heads_here):
        part = slice(h * HEAD_DIM, (h + 1) * HEAD_DIM)
        qh = qkv[0, :, :, part].reshape(length, HEAD_DIM)
        kh = qkv[1, :, :, part].reshape(length, HEAD_DIM)
        vh = qkv[2, :, :, part].reshape(length, HEAD_DIM)
        scores = lax.dot_general(qh, kh, (((1,), (1,)), ((), ())), preferred_element_type=jnp.float32)
        scores = jnp.where(col <= row, scores * HEAD_DIM ** (-0.5), neg_big)
        expo = jnp.exp(scores - jnp.max(scores, axis=1, keepdims=True))
        expo = jnp.where(col <= row, expo, 0.0)
        denom = jnp.sum(expo, axis=1, keepdims=True)
        mixed = jnp.dot(expo.astype(jnp.bfloat16), vh, preferred_element_type=jnp.float32) / denom
        att[:, :, part] = mixed.astype(jnp.bfloat16).reshape(n, toks, HEAD_DIM)

    for d in range(1, n):
        j = lax.rem(z + d, n)
        go(remote(att.at[j], attg.at[0, 0, :, columns(z)], back_s.at[j], back_r.at[z], ctx=j))
    own_att = pltpu.make_async_copy(att.at[z], attg.at[0, 0, :, columns(z)], load_sem.at[8])
    own_att.start()
    own_att.wait()
    for d in range(1, n):
        s = lax.rem(z + d, n)
        here = attg.at[0, 0, :, columns(s)]
        remote(att.at[s], here, back_s.at[s], back_r.at[s], ctx=s).wait_recv()

    go(remote(attg.at[0, 0], attg.at[0, 1], near_s.at[2, 0], near_r.at[2, 0], exp=partner))
    for d in range(1, chips):
        go(remote(attg.at[0, 0], attg.at[d, 0], near_s.at[2, d], near_r.at[2, d], exp=across(d)))

    kinds = (resg, probg, attg)

    def arrived(kind, d, half):
        buf = kinds[kind]
        if half == 0 or d == 0:
            sems = near_s.at[kind, d], near_r.at[kind, d]
        else:
            sems = fwd_s.at[kind, d], fwd_r.at[kind, d]
        remote(buf.at[d, half], buf.at[d, half], *sems, exp=partner).wait_recv()

    def forward(kind, d):
        arrived(kind, d, 0)
        buf = kinds[kind]
        go(remote(buf.at[d, 0], buf.at[d, 1], fwd_s.at[kind, d], fwd_r.at[kind, d], exp=partner))

    for d in range(1, chips):
        forward(0, d)
        forward(1, d)
    own_res.wait()
    for copy in loads:
        copy.wait()
    gain = gain_ref[...]

    def project(d):
        for kind in (0, 1, 2):
            arrived(kind, d, 1)
        rows = attg[d].reshape(2 * toks, -1)
        res = resg[d].reshape(2 * toks, -1).astype(jnp.float32)
        hidden[...] = res + jnp.dot(rows, wo[...], preferred_element_type=jnp.float32)

    def experts(d):
        state = hidden[...]
        mean_square = jnp.mean(state * state, axis=-1, keepdims=True)
        normed = (state * lax.rsqrt(mean_square + 1e-05) * gain).astype(jnp.bfloat16)
        gate = jnp.dot(normed, wg[...], preferred_element_type=jnp.float32)
        up = jnp.dot(normed, wu[...], preferred_element_type=jnp.float32)
        act = (gate / (1.0 + jnp.exp(-gate)) * up).astype(jnp.bfloat16)
        made = jnp.dot(act, wd[...], preferred_element_type=jnp.float32)
        share = probg[d].reshape(2 * toks, -1)
        lane = lax.broadcasted_iota(jnp.int32, share.shape, 1)
        weight = jnp.sum(jnp.where(lane == me, share, 0.0), axis=-1, keepdims=True)
        made = made * weight
        psend[d] = made[toks:].astype(jnp.bfloat16)
        go(remote(psend.at[d], precv.at[d], pair_s.at[d], pair_r.at[d], exp=partner))
        return made[:toks]

    def from_partner(d):
        remote(psend.at[d], precv.at[d], pair_s.at[d], pair_r.at[d], exp=partner).wait_recv()
        return precv[d].astype(jnp.float32)

    def give_back(d):
        ssend[d] = (kept[...] + from_partner(d)).astype(jnp.bfloat16)
        go(remote(ssend.at[d], srecv.at[d], sum_s.at[d], sum_r.at[d], exp=across(d)))

    project(0)
    own[...] = hidden[:toks] + experts(0)
    for d in range(1, chips):
        forward(2, d)
        project(d)
        if d > 1:
            give_back(d - 1)
        kept[...] = experts(d)
    give_back(chips - 1)
    total = own[...] + from_partner(0)
    for d in range(1, chips):
        remote(ssend.at[d], srecv.at[d], sum_s.at[d], sum_r.at[d], exp=partner).wait_recv()
        total = total + srecv[d].astype(jnp.float32)
    out_ref[0] = total.astype(jnp.bfloat16)
    for copy in started:
        copy.wait_send()


def fused(
    n, owners, queries, keys, values, residual, out_proj, norm_gain, w_gate, w_up, w_down, routes, route_prob
):
    chips = owners // 2
    toks, depth = queries.shape[1:]
    model, ffw = w_gate.shape[1:]
    width = depth // n
    lanes = -(-owners // 128) * 128
    bf16, f32 = jnp.bfloat16, jnp.float32
    whole, hbm = pl.BlockSpec(memory_space=pltpu.VMEM), pl.BlockSpec(memory_space=pl.ANY)
    dma = pltpu.SemaphoreType.DMA
    return pl.pallas_call(
        functools.partial(fused_kernel, n, chips),
        out_shape=jax.ShapeDtypeStruct((1, toks, model), bf16),
        in_specs=[hbm, hbm, hbm, hbm, hbm, whole, hbm, hbm, hbm, whole, whole],
        out_specs=whole,
        scratch_shapes=[
            pltpu.VMEM((3, n, toks, width), bf16),
            pltpu.VMEM((n, toks, width), bf16),
            pltpu.VMEM((chips, 2, toks, depth), bf16),
            pltpu.VMEM((chips, 2, toks, model), bf16),
            pltpu.VMEM((chips, 2, toks, lanes), f32),
            pltpu.VMEM((depth, model), bf16),
            pltpu.VMEM((model, ffw), bf16),
            pltpu.VMEM((model, ffw), bf16),
            pltpu.VMEM((ffw, model), bf16),
            pltpu.VMEM((toks, model), f32),
            pltpu.VMEM((2 * toks, model), f32),
            pltpu.VMEM((toks, model), f32),
            pltpu.VMEM((chips, toks, model), bf16),
            pltpu.VMEM((chips, toks, model), bf16),
            pltpu.VMEM((chips, toks, model), bf16),
            pltpu.VMEM((chips, toks, model), bf16),
            dma((9,)),
            dma((3, n)), dma((3, n)),
            dma((n,)), dma((n,)),
            dma((3, chips)), dma((3, chips)),
            dma((3, chips)), dma((3, chips)),
            dma((chips,)), dma((chips,)),
            dma((chips,)), dma((chips,)),
        ],
        compiler_params=pltpu.CompilerParams(
            collective_id=0, has_side_effects=True, vmem_limit_bytes=48 * 1024 * 1024
        ),
    )(
        queries, keys, values, residual, out_proj, norm_gain.reshape(1, -1), w_gate, w_up, w_down,
        routes, route_prob,
    )


def solution(mesh):
    placed = (
        P("exp", "ctx", None),
        P("exp", "ctx", None),
        P("exp", "ctx", None),
        P("exp", "ctx", None),
        P(),
        P(),
        P("exp", None, None),
        P("exp", None, None),
        P("exp", None, None),
        P("exp", "ctx", None),
        P("exp", "ctx", None),
    )
    n, owners = mesh.shape["ctx"], mesh.shape["exp"]
    chips = owners // 2
    splits = HEADS % n == 0 and owners % 2 == 0 and chips & (chips - 1) == 0
    step = functools.partial(fused, n, owners) if splits else local
    return jax.shard_map(
        step, mesh=mesh, in_specs=placed, out_specs=P("exp", "ctx", None), check_vma=False
    )
```

```python
import functools

import jax
import jax.numpy as jnp
from jax import lax
from jax.experimental import pallas as pl
from jax.experimental.pallas import tpu as pltpu
from jax.sharding import PartitionSpec as P

HEADS = 8
HEAD_DIM = 128
TOP = 4


neg_big = -1e30


def passed_along(block, axis, distance):
    devices = range(lax.axis_size(axis))
    route = [(i - distance, i) for i in devices if i - distance in devices]
    return lax.ppermute(block, axis, route)


def attend_piece(softmax_state, query_heads, query_pos, key_piece, piece_start):
    run_max, run_sum, run_acc = softmax_state
    length = key_piece.shape[1]
    key_rows = key_piece[0].reshape(length, HEADS, HEAD_DIM)
    value_rows = key_piece[1].reshape(length, HEADS, HEAD_DIM)
    scale = HEAD_DIM ** (-0.5)
    scores = jnp.einsum("hqd,khd->hqk", query_heads, key_rows, preferred_element_type=jnp.float32)
    key_pos = piece_start + jnp.arange(length, dtype=jnp.int32)
    allowed = key_pos[None, :] <= query_pos[:, None]
    scores = jnp.where(allowed[None], scores, neg_big)
    new_max = jnp.maximum(run_max, scores.max(axis=-1))
    rescale = jnp.exp((run_max - new_max) * scale)
    exponent = jnp.where(allowed[None], jnp.exp((scores - new_max[:, :, None]) * scale), 0.0)
    run_sum = run_sum * rescale + exponent.sum(axis=-1)
    update = jnp.einsum(
        "hqk,khd->hqd",
        exponent.astype(jnp.bfloat16),
        value_rows,
        preferred_element_type=jnp.float32,
    )
    run_acc = run_acc * rescale[:, :, None] + update
    return (new_max, run_sum, run_acc)


def local(
    queries, keys, values, residual, out_proj, norm_gain, w_gate, w_up, w_down, routes, route_prob
):
    tok_count = queries.shape[1]
    my_index = lax.axis_index("ctx")
    query_pos = my_index * tok_count + jnp.arange(tok_count, dtype=jnp.int32)
    query_heads = jnp.transpose(queries[0].reshape(tok_count, HEADS, HEAD_DIM), (1, 0, 2))
    stacked = jnp.stack([keys[0], values[0]])
    start_state = (
        jnp.full((HEADS, tok_count), neg_big, jnp.float32),
        jnp.zeros((HEADS, tok_count), jnp.float32),
        jnp.zeros((HEADS, tok_count, HEAD_DIM), jnp.float32),
    )
    first_state = attend_piece(start_state, query_heads, query_pos, stacked, my_index * tok_count)

    def advance(offset, loop_carry):
        softmax_state, travelling = loop_carry
        travelling = passed_along(travelling, "ctx", 1)

        def compute(current):
            return attend_piece(
                current, query_heads, query_pos, travelling, (my_index - offset) * tok_count
            )

        def unchanged(current):
            return current

        softmax_state = lax.cond(offset <= my_index, compute, unchanged, softmax_state)
        return (softmax_state, travelling)

    final_state, leftover = lax.fori_loop(1, lax.axis_size("ctx"), advance, (first_state, stacked))
    run_max, run_sum, run_acc = final_state
    attended_heads = (run_acc / run_sum[:, :, None]).astype(jnp.bfloat16)
    attended = jnp.transpose(attended_heads, (1, 0, 2)).reshape(tok_count, HEADS * HEAD_DIM)
    hidden = residual[0].astype(jnp.float32) + jnp.dot(
        attended, out_proj, preferred_element_type=jnp.float32
    )
    mean_square = jnp.mean(hidden * hidden, axis=-1, keepdims=True)
    normed = (hidden * lax.rsqrt(mean_square + 1e-05) * norm_gain).astype(jnp.bfloat16)
    owners = lax.axis_size("exp")
    capacity = 3 * tok_count * TOP // (2 * owners)
    chosen = routes[0].reshape(-1)
    one_hot = (chosen[:, None] == jnp.arange(owners, dtype=jnp.int32)[None, :]).astype(jnp.int32)
    earlier = jnp.cumsum(one_hot, axis=0) - one_hot
    slot_index = jnp.sum(earlier * one_hot, axis=1)
    target = chosen * capacity + slot_index
    token_index = jnp.arange(tok_count * TOP, dtype=jnp.int32) // TOP
    slot_token = jnp.full((owners * capacity,), tok_count, jnp.int32).at[target].set(token_index)
    padded = jnp.concatenate([normed, jnp.zeros((1, normed.shape[1]), jnp.bfloat16)], axis=0)
    outgoing = padded[slot_token].reshape(owners, capacity, normed.shape[1])
    incoming = lax.all_to_all(outgoing, "exp", split_axis=0, concat_axis=0, tiled=True)
    sources, item_count, feature_width = incoming.shape
    flat_rows = incoming.reshape(sources * item_count, feature_width)
    gate_part = jnp.dot(flat_rows, w_gate[0], preferred_element_type=jnp.float32)
    up_part = jnp.dot(flat_rows, w_up[0], preferred_element_type=jnp.float32)
    activated = (jax.nn.silu(gate_part) * up_part).astype(jnp.bfloat16)
    produced = jnp.dot(activated, w_down[0], preferred_element_type=jnp.float32).astype(
        jnp.bfloat16
    )
    produced = produced.reshape(sources, item_count, feature_width)
    returned = lax.all_to_all(produced, "exp", split_axis=0, concat_axis=0, tiled=True)
    picked = (
        returned.reshape(owners * capacity, -1)[target]
        .astype(jnp.float32)
        .reshape(tok_count, TOP, -1)
    )
    mixture = jnp.sum(route_prob[0][:, :, None] * picked, axis=1)
    return (hidden + mixture).astype(jnp.bfloat16)[None]


MESH = pl.DeviceIdType.MESH


def fused_kernel(
    n, chips, q_hbm, k_hbm, v_hbm, res_hbm, wo_hbm, gain_ref, wg_hbm, wu_hbm, wd_hbm, routes_ref, prob_ref,
    out_ref,
    qkv, att, attg, resg, probg, wo, wg, wu, wd, kept, hidden, own, psend, precv, ssend, srecv,
    load_sem, qkv_s, qkv_r, back_s, back_r, att_s, att_r, near_s, near_r, fwd_s, fwd_r, pair_s, pair_r, sum_s, sum_r,
):
    z = lax.axis_index("ctx")
    me = lax.axis_index("exp")
    core = lax.rem(me, 2)
    chip = me // 2
    partner = me + 1 - 2 * core
    toks = q_hbm.shape[1]
    width = qkv.shape[-1]
    heads_here = width // HEAD_DIM

    def across(d):
        there = chip
        for b in range(chips.bit_length() - 1):
            if (d >> b) & 1:
                there = there + (1 << b) * (1 - 2 * lax.rem(chip // (1 << b), 2))
        return 2 * there + core

    def remote(src, dst, ssem, rsem, **to):
        return pltpu.make_async_remote_copy(
            src_ref=src, dst_ref=dst, send_sem=ssem, recv_sem=rsem, device_id=to, device_id_type=MESH
        )

    def columns(j):
        return pl.ds(pl.multiple_of(j * width, width), width)

    sources = (q_hbm, k_hbm, v_hbm)
    started = []

    def go(copy):
        copy.start()
        started.append(copy)
        return copy

    own_qkv = []
    for t in range(3):
        own_qkv.append(pltpu.make_async_copy(sources[t].at[0, :, columns(z)], qkv.at[t, z], load_sem.at[t]))
        own_qkv[-1].start()
    own_res = pltpu.make_async_copy(res_hbm.at[0], resg.at[0, 0], load_sem.at[3])
    own_res.start()
    loads = []
    for i, (src, dst) in enumerate(((wo_hbm, wo), (wg_hbm.at[0], wg), (wu_hbm.at[0], wu), (wd_hbm.at[0], wd))):
        loads.append(pltpu.make_async_copy(src, dst, load_sem.at[4 + i]))
        loads[-1].start()

    barrier = pltpu.get_barrier_semaphore()
    for d in range(1, n):
        pl.semaphore_signal(barrier, inc=1, device_id={"ctx": lax.rem(z + d, n)}, device_id_type=MESH)
    for d in range(1, chips):
        pl.semaphore_signal(barrier, inc=1, device_id={"exp": across(d)}, device_id_type=MESH)
    pl.semaphore_signal(barrier, inc=1, device_id={"exp": partner}, device_id_type=MESH)
    pl.semaphore_wait(barrier, n - 1 + chips)

    for t in range(3):
        for d in range(1, n):
            j = lax.rem(z + d, n)
            go(remote(sources[t].at[0, :, columns(j)], qkv.at[t, z], qkv_s.at[t, j], qkv_r.at[t, z], ctx=j))
    go(remote(res_hbm.at[0], resg.at[0, 1], near_s.at[0, 0], near_r.at[0, 0], exp=partner))
    for d in range(1, chips):
        go(remote(res_hbm.at[0], resg.at[d, 0], near_s.at[0, d], near_r.at[0, d], exp=across(d)))
    lanes = lax.broadcasted_iota(jnp.int32, probg.shape[2:], 1)
    dense = jnp.zeros(probg.shape[2:], jnp.float32)
    for t in range(TOP):
        dense = dense + jnp.where(lanes == routes_ref[0, :, t : t + 1], prob_ref[0, :, t : t + 1], 0.0)
    probg[0, 0] = dense
    go(remote(probg.at[0, 0], probg.at[0, 1], near_s.at[1, 0], near_r.at[1, 0], exp=partner))
    for d in range(1, chips):
        go(remote(probg.at[0, 0], probg.at[d, 0], near_s.at[1, d], near_r.at[1, d], exp=across(d)))

    def collected(t):
        own_qkv[t].wait()
        for d in range(1, n):
            s = lax.rem(z + d, n)
            remote(qkv.at[t, s], qkv.at[t, s], qkv_s.at[t, s], qkv_r.at[t, s], ctx=s).wait_recv()

    collected(0)
    collected(1)
    length = n * toks
    row = lax.broadcasted_iota(jnp.int32, (length, length), 0)
    col = lax.broadcasted_iota(jnp.int32, (length, length), 1)
    parts = [slice(h * HEAD_DIM, (h + 1) * HEAD_DIM) for h in range(heads_here)]
    soft = []
    for part in parts:
        qh = qkv[0, :, :, part].reshape(length, HEAD_DIM)
        kh = qkv[1, :, :, part].reshape(length, HEAD_DIM)
        scores = lax.dot_general(qh, kh, (((1,), (1,)), ((), ())), preferred_element_type=jnp.float32)
        scores = jnp.where(col <= row, scores * HEAD_DIM ** (-0.5), neg_big)
        expo = jnp.exp(scores - jnp.max(scores, axis=1, keepdims=True))
        expo = jnp.where(col <= row, expo, 0.0)
        soft.append((expo.astype(jnp.bfloat16), jnp.sum(expo, axis=1, keepdims=True)))
    collected(2)
    for part, (expo, denom) in zip(parts, soft):
        vh = qkv[2, :, :, part].reshape(length, HEAD_DIM)
        mixed = jnp.dot(expo, vh, preferred_element_type=jnp.float32) / denom
        att[:, :, part] = mixed.astype(jnp.bfloat16).reshape(n, toks, HEAD_DIM)

    def share(src, s):
        go(remote(src, attg.at[0, 1, :, columns(s)], att_s.at[s, 0], att_r.at[s, 0], exp=partner))
        for d in range(1, chips):
            go(remote(src, attg.at[d, 0, :, columns(s)], att_s.at[s, d], att_r.at[s, d], exp=across(d)))

    for d in range(1, n):
        j = lax.rem(z + d, n)
        go(remote(att.at[j], attg.at[0, 0, :, columns(z)], back_s.at[j], back_r.at[z], ctx=j))
    own_att = pltpu.make_async_copy(att.at[z], attg.at[0, 0, :, columns(z)], load_sem.at[8])
    own_att.start()
    share(att.at[z], z)
    for d in sorted(range(1, n), key=lambda d: min(d, n - d)):
        s = lax.rem(z + d, n)
        here = attg.at[0, 0, :, columns(s)]
        remote(att.at[s], here, back_s.at[s], back_r.at[s], ctx=s).wait_recv()
        share(here, s)
    own_att.wait()

    kinds = (resg, probg, attg)

    def arrived(kind, d, half):
        buf = kinds[kind]
        if kind == 2 and (half == 0 or d == 0):
            for i in range(n):
                s = lax.rem(z + i, n)
                here = buf.at[d, half, :, columns(s)]
                remote(here, here, att_s.at[s, d], att_r.at[s, d], exp=partner).wait_recv()
            return
        if half == 0 or d == 0:
            sems = near_s.at[kind, d], near_r.at[kind, d]
        else:
            sems = fwd_s.at[kind, d], fwd_r.at[kind, d]
        remote(buf.at[d, half], buf.at[d, half], *sems, exp=partner).wait_recv()

    def forward(kind, d):
        arrived(kind, d, 0)
        buf = kinds[kind]
        go(remote(buf.at[d, 0], buf.at[d, 1], fwd_s.at[kind, d], fwd_r.at[kind, d], exp=partner))

    own_res.wait()
    for copy in loads:
        copy.wait()
    gain = gain_ref[...]

    def project(lo, hi):
        for d in range(lo, hi):
            for kind in (0, 1, 2):
                arrived(kind, d, 1)
        count = 2 * toks * (hi - lo)
        rows = attg[lo:hi].reshape(count, -1)
        res = resg[lo:hi].reshape(count, -1).astype(jnp.float32)
        hidden[:count] = res + jnp.dot(rows, wo[...], preferred_element_type=jnp.float32)

    def experts(lo, hi):
        count = 2 * toks * (hi - lo)
        state = hidden[:count]
        mean_square = jnp.mean(state * state, axis=-1, keepdims=True)
        normed = (state * lax.rsqrt(mean_square + 1e-05) * gain).astype(jnp.bfloat16)
        gate = jnp.dot(normed, wg[...], preferred_element_type=jnp.float32)
        up = jnp.dot(normed, wu[...], preferred_element_type=jnp.float32)
        act = (gate / (1.0 + jnp.exp(-gate)) * up).astype(jnp.bfloat16)
        made = jnp.dot(act, wd[...], preferred_element_type=jnp.float32)
        share = probg[lo:hi].reshape(count, -1)
        lane = lax.broadcasted_iota(jnp.int32, share.shape, 1)
        weight = jnp.sum(jnp.where(lane == me, share, 0.0), axis=-1, keepdims=True)
        made = (made * weight).reshape(hi - lo, 2, toks, -1)
        for d in range(lo, hi):
            psend[d] = made[d - lo, 1].astype(jnp.bfloat16)
            go(remote(psend.at[d], precv.at[d], pair_s.at[d], pair_r.at[d], exp=partner))
        kept[lo:hi] = made[:, 0]

    def from_partner(d):
        remote(psend.at[d], precv.at[d], pair_s.at[d], pair_r.at[d], exp=partner).wait_recv()
        return precv[d].astype(jnp.float32)

    def give_back(d):
        ssend[d] = (kept[d] + from_partner(d)).astype(jnp.bfloat16)
        go(remote(ssend.at[d], srecv.at[d], sum_s.at[d], sum_r.at[d], exp=across(d)))

    project(0, 1)
    own[...] = hidden[:toks]
    for d in range(1, chips):
        forward(0, d)
        forward(1, d)
    experts(0, 1)
    before = range(0)
    for lo in range(1, chips, 2):
        hi = min(lo + 2, chips)
        for d in range(lo, hi):
            forward(2, d)
        project(lo, hi)
        for d in before:
            give_back(d)
        experts(lo, hi)
        before = range(lo, hi)
    for d in before:
        give_back(d)
    total = own[...] + kept[0] + from_partner(0)
    for d in range(1, chips):
        remote(ssend.at[d], srecv.at[d], sum_s.at[d], sum_r.at[d], exp=partner).wait_recv()
        total = total + srecv[d].astype(jnp.float32)
    out_ref[0] = total.astype(jnp.bfloat16)
    for copy in started:
        copy.wait_send()


def fused(
    n, owners, queries, keys, values, residual, out_proj, norm_gain, w_gate, w_up, w_down, routes, route_prob
):
    chips = owners // 2
    toks, depth = queries.shape[1:]
    model, ffw = w_gate.shape[1:]
    width = depth // n
    lanes = -(-owners // 128) * 128
    bf16, f32 = jnp.bfloat16, jnp.float32
    whole, hbm = pl.BlockSpec(memory_space=pltpu.VMEM), pl.BlockSpec(memory_space=pltpu.HBM)
    dma = pltpu.SemaphoreType.DMA
    return pl.pallas_call(
        functools.partial(fused_kernel, n, chips),
        out_shape=jax.ShapeDtypeStruct((1, toks, model), bf16),
        in_specs=[hbm, hbm, hbm, hbm, hbm, whole, hbm, hbm, hbm, whole, whole],
        out_specs=whole,
        scratch_shapes=[
            pltpu.VMEM((3, n, toks, width), bf16),
            pltpu.VMEM((n, toks, width), bf16),
            pltpu.VMEM((chips, 2, toks, depth), bf16),
            pltpu.VMEM((chips, 2, toks, model), bf16),
            pltpu.VMEM((chips, 2, toks, lanes), f32),
            pltpu.VMEM((depth, model), bf16),
            pltpu.VMEM((model, ffw), bf16),
            pltpu.VMEM((model, ffw), bf16),
            pltpu.VMEM((ffw, model), bf16),
            pltpu.VMEM((chips, toks, model), f32),
            pltpu.VMEM((4 * toks, model), f32),
            pltpu.VMEM((toks, model), f32),
            pltpu.VMEM((chips, toks, model), bf16),
            pltpu.VMEM((chips, toks, model), bf16),
            pltpu.VMEM((chips, toks, model), bf16),
            pltpu.VMEM((chips, toks, model), bf16),
            dma((9,)),
            dma((3, n)), dma((3, n)),
            dma((n,)), dma((n,)),
            dma((n, chips)), dma((n, chips)),
            dma((3, chips)), dma((3, chips)),
            dma((3, chips)), dma((3, chips)),
            dma((chips,)), dma((chips,)),
            dma((chips,)), dma((chips,)),
        ],
        compiler_params=pltpu.CompilerParams(
            collective_id=0, has_side_effects=True, vmem_limit_bytes=48 * 1024 * 1024
        ),
    )(
        queries, keys, values, residual, out_proj, norm_gain.reshape(1, -1), w_gate, w_up, w_down,
        routes, route_prob,
    )


def solution(mesh):
    placed = (
        P("exp", "ctx", None),
        P("exp", "ctx", None),
        P("exp", "ctx", None),
        P("exp", "ctx", None),
        P(),
        P(),
        P("exp", None, None),
        P("exp", None, None),
        P("exp", None, None),
        P("exp", "ctx", None),
        P("exp", "ctx", None),
    )
    n, owners = mesh.shape["ctx"], mesh.shape["exp"]
    chips = owners // 2
    splits = HEADS % n == 0 and owners % 2 == 0 and chips & (chips - 1) == 0
    step = functools.partial(fused, n, owners) if splits else local
    return jax.shard_map(
        step, mesh=mesh, in_specs=placed, out_specs=P("exp", "ctx", None), check_vma=False
    )
```
